512 devices in a mesh: rows: 32 (over y, x), sub: 16 (over z, core).
Axes of the slice: x: 4, y: 8, z: 8, core: 2. Of those that a mesh axis runs over, the one named last changes fastest.
Arguments:
- slab: bfloat16 [131072, 1024], P(('rows', 'sub')), may hold values from -6 to 6
- lower_bound: float32 [1], replicated, may hold values from 0.3 to 0.7
Outputs:
- panel_out: float32 [131072, 1024], P(('rows', 'sub'))
- checksum_out: float32 [512, 1024], P(('rows', 'sub'))
The draws below stay inside these ranges and needn't reach their ends.
All inputs are finite; a program needn't handle non-finite values.
Results may differ from the reference program's by a relative error of at most 0.0017.
The reference program's roundings to bfloat16 on the way (of `inverse_half` and `projected`) count: a program that leaves them out, or rounds other values in their place, can miss the bound.
Values sent between devices are 32-bit elements; how exact they have to be, the bound alone decides.
No kernel may reach another device: no remote copies, remote signals or barrier semaphores. Data moves between devices by JAX's collectives and lax.ppermute only.
A program may use at most 128 MiB of HBM per device.

```python
import math
import jax
import jax.numpy as jnp
from jax import lax

WIDTH = 1024
ROWS_DEV = 256
ROWS = 131072


def rotate_pairs(matrix, angles):
    row_count, column_count = matrix.shape
    paired = matrix.reshape(row_count, column_count // 2, 2)
    cosine = jnp.cos(angles)[None, :]
    sine_part = jnp.sin(angles)[None, :]
    first_half = paired[:, :, 0]
    second_half = paired[:, :, 1]
    turned = jnp.stack([cosine * first_half - sine_part * second_half, sine_part * first_half + cosine * second_half], axis=-1)
    return turned.reshape(row_count, column_count)


def mix_columns(matrix, angle_key, layer_count):
    column_count = matrix.shape[1]
    for layer in range(layer_count):
        angles = jax.random.uniform(jax.random.fold_in(angle_key, layer), (column_count // 2,), jnp.float32, -math.pi, math.pi)
        if layer % 2 == 1:
            matrix = jnp.roll(rotate_pairs(jnp.roll(matrix, -1, axis=1), angles), 1, axis=1)
        else:
            matrix = rotate_pairs(matrix, angles)
    return matrix


def draw_slab(key, part):
    key = jax.random.fold_in(key, 11)
    field_key = jax.random.fold_in(key, 1)
    scale_key = jax.random.fold_in(key, 2)
    angle_key = jax.random.fold_in(key, 3)
    column_scales = jnp.exp(jax.random.uniform(scale_key, (WIDTH,), jnp.float32, math.log(0.1), 0.0))
    random_part = jax.random.normal(field_key, (ROWS, WIDTH), jnp.float32)
    layer_count = 16
    mixed_field = mix_columns(random_part * column_scales[None, :], angle_key, layer_count)
    return jnp.clip(mixed_field, -6.0, 6.0).astype(jnp.bfloat16)


def setup_inputs(seed: int = 0) -> dict:
    arg_keys = jax.random.split(jax.random.key(seed), 3)
    slab = draw_slab(jax.random.fold_in(arg_keys[2], 71), 0)
    lower_bound = jnp.clip(jnp.exp(jax.random.uniform(arg_keys[1], (1,), jnp.float32, math.log(0.3), math.log(0.7))), 0.3, 0.7)
    return {"slab": slab, "lower_bound": lower_bound}


def qdwh_weights(lower_bound):
    value = lower_bound[0].astype(jnp.float32)
    square = value * value
    delta = jnp.cbrt(4.0 * (1.0 - square) / (square * square))
    root = jnp.sqrt(1.0 + delta)
    alpha = root + 0.5 * jnp.sqrt(8.0 - 4.0 * delta + 8.0 * (2.0 - square) / (square * root))
    beta = (alpha - 1.0) ** 2 / 4.0
    shift = alpha + beta - 1.0
    return (beta / shift, alpha - beta / shift, shift)

def reference(slab, lower_bound):
    rows_all = slab.shape[0]
    width = slab.shape[1]
    matrix = slab.astype(jnp.float32)
    gram = jnp.dot(matrix.T, matrix, precision=lax.Precision.HIGHEST) / rows_all
    first, second, shift = qdwh_weights(lower_bound)
    identity = jnp.eye(width, dtype=jnp.float32)
    shifted = identity + shift * gram
    factor = jnp.linalg.cholesky(shifted)
    inverse = lax.linalg.triangular_solve(factor, identity, left_side=True, lower=True)
    inverse_half = inverse.astype(jnp.bfloat16)
    projected = jnp.dot(slab.astype(jnp.float32), inverse_half.T.astype(jnp.float32), preferred_element_type=jnp.float32).astype(jnp.bfloat16)
    solved = jnp.dot(projected.astype(jnp.float32), inverse_half.astype(jnp.float32), preferred_element_type=jnp.float32)
    panel_out = first * matrix + second * solved
    checksum = lax.optimization_barrier(jnp.sum(matrix.reshape(-1, ROWS_DEV, width), axis=1)) / math.sqrt(ROWS_DEV)
    check_solved = jnp.dot(jnp.dot(checksum, inverse.T, precision=lax.Precision.HIGHEST), inverse, precision=lax.Precision.HIGHEST)
    checksum_out = first * checksum + second * check_solved
    return (panel_out, checksum_out)
```

```python
import jax
import jax.numpy as jnp
from jax import lax
from jax.experimental import pallas as pl
from jax.experimental.pallas import tpu as pltpu
from jax.sharding import Mesh
from jax.sharding import PartitionSpec as P

WIDTH = 1024
BLOCK = 128
COUNT = WIDTH // BLOCK
PAIRS = COUNT * (COUNT + 1) // 2
HALF = PAIRS // 2
HALF_ROWS = HALF * BLOCK
BASE = 32


def qdwh_weights(lower_bound):
    value = lower_bound[0]
    square = value * value
    delta = jnp.cbrt(4.0 * (1.0 - square) / (square * square))
    root = jnp.sqrt(1.0 + delta)
    alpha = root + 0.5 * jnp.sqrt(8.0 - 4.0 * delta + 8.0 * (2.0 - square) / (square * root))
    beta = (alpha - 1.0) ** 2 / 4.0
    shift = alpha + beta - 1.0
    return (beta / shift, alpha - beta / shift, shift)


def iota(shape, dimension):
    return lax.broadcasted_iota(jnp.int32, shape, dimension)


def dot_nn(left, right):
    return jnp.dot(left, right, preferred_element_type=jnp.float32)


def dot_nt(left, right):
    return lax.dot_general(
        left, right, (((1,), (1,)), ((), ())), preferred_element_type=jnp.float32
    )


def dot_tn(left, right):
    return lax.dot_general(
        left, right, (((0,), (0,)), ((), ())), preferred_element_type=jnp.float32
    )


def split(value):
    high = value.astype(jnp.bfloat16)
    rest = value - high.astype(jnp.float32)
    middle = rest.astype(jnp.bfloat16)
    low = (rest - middle.astype(jnp.float32)).astype(jnp.bfloat16)
    return high, middle, low


def left_terms(value, axis):
    high, middle, low = split(value)
    return jnp.concatenate([high, high, middle, high, low, middle], axis=axis)


def right_terms(value, axis):
    high, middle, low = split(value)
    return jnp.concatenate([high, middle, high, low, high, middle], axis=axis)


def block_pairs():
    return [(row, column) for row in range(COUNT) for column in range(row, COUNT)]


def gram_kernel(slab_ref, mine_ref, other_ref):
    core = lax.axis_index("core")
    for side in range(2):

        @pl.when(core == side)
        def _():
            position = 0
            for row in range(COUNT):
                product = dot_tn(
                    slab_ref[:, row * BLOCK : (row + 1) * BLOCK], slab_ref[:, row * BLOCK :]
                )
                for step in range(COUNT - row):
                    half, place = divmod(position, HALF)
                    target = mine_ref if half == side else other_ref
                    target[place * BLOCK : (place + 1) * BLOCK, :] = product[
                        :, step * BLOCK : (step + 1) * BLOCK
                    ]
                    position += 1


def gram_blocks(slab):
    shape = jax.ShapeDtypeStruct((HALF_ROWS, BLOCK), jnp.float32)
    return pl.pallas_call(
        gram_kernel,
        out_shape=(shape, shape),
        in_specs=[pl.BlockSpec(memory_space=pltpu.VMEM)],
        out_specs=(pl.BlockSpec(memory_space=pltpu.VMEM),) * 2,
        compiler_params=pltpu.CompilerParams(vmem_limit_bytes=32 * 2**20),
    )(slab)


def eliminate(row, offset):
    groups = BASE // 8
    lane = iota((8, BLOCK), 1)
    sub = iota((8, BLOCK), 0)
    columns = []
    for column in range(BASE):
        columns.append(
            [
                None
                if group < column // 8
                else jnp.broadcast_to(
                    row[8 * group : 8 * group + 8, offset + column : offset + column + 1],
                    (8, BLOCK),
                )
                for group in range(groups)
            ]
        )
    result = []
    for group in range(groups):
        eye = jnp.where(lane == sub + (offset + 8 * group), 1.0, 0.0)
        inside = (lane >= offset) & (lane < offset + BASE)
        result.append(jnp.where(inside, eye, row[8 * group : 8 * group + 8]))
    pivots = [jnp.ones((8, BLOCK), jnp.float32) for _ in range(groups)]

    def spread(value, sublane):
        return jnp.broadcast_to(value[sublane : sublane + 1], (8, BLOCK))

    for column in range(BASE):
        home, sublane = divmod(column, 8)
        current = columns[column]
        pivot = spread(current[home], sublane)
        inverse_pivot = 1.0 / pivot
        pivots[home] = jnp.where(sub == sublane, pivot, pivots[home])
        scaled = [None] * groups
        for group in range(home, groups):
            scaled[group] = current[group] * inverse_pivot
        for later in range(column + 1, BASE):
            factor = spread(current[later // 8], later % 8)
            for group in range(later // 8, groups):
                columns[later][group] = columns[later][group] - scaled[group] * factor
        source = spread(result[home], sublane)
        for group in range(home, groups):
            multiplier = scaled[group]
            if group == home:
                if sublane == 7:
                    continue
                multiplier = jnp.where(sub > sublane, multiplier, 0.0)
            result[group] = result[group] - multiplier * source
    return jnp.concatenate(
        [result[group] * lax.rsqrt(pivots[group]) for group in range(groups)], axis=0
    )


def inverse_factor_block(block):
    count = BLOCK // BASE
    rows = [block[BASE * index : BASE * (index + 1)] for index in range(count)]
    lane = iota((BASE, BLOCK), 1)
    out = []
    for index in range(count):
        start = BASE * index
        done = eliminate(rows[index], start)
        out.append(jnp.where(lane < start + BASE, done, 0.0))
        if index + 1 < count:
            update = dot_tn(left_terms(done, 0), right_terms(done, 0))
            for later in range(index + 1, count):
                kept = jnp.where((lane >= start) & (lane < start + BASE), 0.0, rows[later])
                rows[later] = kept - update[BASE * later : BASE * (later + 1)]
    return jnp.concatenate(out, axis=0)


def step_kernel(
    weights_ref, mine_ref, other_ref, slab_ref, out_ref, check_ref,
    matrix, panel, terms, solved, checksum, checked,
):
    core = lax.axis_index("core")
    first, second, scale = weights_ref[0], weights_ref[1], weights_ref[2]
    diagonal = jnp.where(iota((BLOCK, BLOCK), 0) == iota((BLOCK, BLOCK), 1), 1.0, 0.0)
    matrix[...] = jnp.zeros_like(matrix)
    for side in range(2):

        @pl.when(core == side)
        def _():
            for position, (row, column) in enumerate(block_pairs()):
                half, place = divmod(position, HALF)
                source = mine_ref if half == side else other_ref
                value = source[place * BLOCK : (place + 1) * BLOCK, :] * scale
                if row == column:
                    value = value + diagonal
                matrix[
                    row * BLOCK : (row + 1) * BLOCK, column * BLOCK : (column + 1) * BLOCK
                ] = value

    column_block = iota((BLOCK, WIDTH), 1) // BLOCK
    rows_dev = slab_ref.shape[0]
    checksum[...] = jnp.broadcast_to(
        jnp.sum(slab_ref[...].astype(jnp.float32), axis=0, keepdims=True) / (rows_dev**0.5),
        checksum.shape,
    )
    checked[...] = jnp.zeros_like(checked)
    solved[...] = jnp.zeros_like(solved)

    def step(index, carry):
        here = pl.ds(pl.multiple_of(index * BLOCK, BLOCK), BLOCK)
        inverse_block = inverse_factor_block(matrix[here, here])
        panel[...] = dot_nn(left_terms(inverse_block, 1), right_terms(matrix[here, :], 0))
        panel[:, here] = inverse_block
        value = panel[...]
        terms[...] = right_terms(value, 0)

        def update(later, carry):
            there = pl.ds(pl.multiple_of(later * BLOCK, BLOCK), BLOCK)
            left = left_terms(panel[:, there].T, 1)
            kept = jnp.where(column_block == index, 0.0, matrix[there, :])
            matrix[there, :] = kept - dot_nn(left, terms[...])
            return carry

        lax.fori_loop(index + 1, COUNT, update, 0)
        inverse = jnp.where(column_block <= index, value, 0.0)
        inverse_half = inverse.astype(jnp.bfloat16)
        projected = dot_nt(slab_ref[...], inverse_half).astype(jnp.bfloat16)
        solved[...] += dot_nn(projected, inverse_half)
        weight = jnp.sum(inverse * checksum[0:1, :], axis=1, keepdims=True)
        checked[...] += (inverse * weight).reshape(BLOCK // 8, 8, WIDTH).sum(axis=0)
        return carry

    lax.fori_loop(0, COUNT, step, 0)
    out_ref[...] = first * slab_ref[...].astype(jnp.float32) + second * solved[...]
    check_ref[...] = first * checksum[0:1, :] + second * jnp.sum(
        checked[...], axis=0, keepdims=True
    )


def polar_step(weights, mine, other, slab):
    rows_dev = slab.shape[0]
    vmem = pl.BlockSpec(memory_space=pltpu.VMEM)
    return pl.pallas_call(
        step_kernel,
        out_shape=(
            jax.ShapeDtypeStruct((rows_dev, WIDTH), jnp.float32),
            jax.ShapeDtypeStruct((1, WIDTH), jnp.float32),
        ),
        in_specs=[pl.BlockSpec(memory_space=pltpu.SMEM), vmem, vmem, vmem],
        out_specs=(vmem, vmem),
        scratch_shapes=[
            pltpu.VMEM((WIDTH, WIDTH), jnp.float32),
            pltpu.VMEM((BLOCK, WIDTH), jnp.float32),
            pltpu.VMEM((6 * BLOCK, WIDTH), jnp.bfloat16),
            pltpu.VMEM((rows_dev, WIDTH), jnp.float32),
            pltpu.VMEM((8, WIDTH), jnp.float32),
            pltpu.VMEM((8, WIDTH), jnp.float32),
        ],
        compiler_params=pltpu.CompilerParams(vmem_limit_bytes=48 * 2**20),
    )(weights, mine, other, slab)


def exchange(parts, axis):
    return lax.all_to_all(parts, axis, 0, 0, tiled=True)


def shared(part, count):
    return jnp.broadcast_to(part[None], (count,) + part.shape)


def swap(value):
    return lax.ppermute(value, "core", [(0, 1), (1, 0)])


def sum_over_devices(mine, other):
    size_x, size_y, size_z = (lax.axis_size(name) for name in ("x", "y", "z"))
    own = mine + swap(other)
    own = exchange(own.reshape(size_x, -1, BLOCK), "x").sum(axis=0)
    own = exchange(own.reshape(size_y, -1, BLOCK), "y").sum(axis=0)
    own = exchange(shared(own, size_z), "z").sum(axis=0)
    own = exchange(shared(own, size_y), "y").reshape(-1, BLOCK)
    own = exchange(shared(own, size_x), "x").reshape(-1, BLOCK)
    return own, swap(own)


def per_device(slab, lower_bound):
    devices_all = 1
    for name in ("y", "x", "z", "core"):
        devices_all *= lax.axis_size(name)
    first, second, shift = qdwh_weights(lower_bound)
    weights = jnp.stack([first, second, shift / (slab.shape[0] * devices_all)])
    mine, other = sum_over_devices(*gram_blocks(slab))
    return polar_step(weights, mine, other, slab)


def solution(mesh):
    names = ("y", "x", "z", "core")
    wide = Mesh(mesh.devices.reshape(8, 4, 8, 2), names)
    return jax.shard_map(
        per_device,
        mesh=wide,
        in_specs=(P(names, None), P()),
        out_specs=(P(names, None), P(names, None)),
        check_vma=False,
    )
```

```python
import jax
import jax.numpy as jnp
from jax import lax
from jax.experimental import pallas as pl
from jax.experimental.pallas import tpu as pltpu
from jax.sharding import Mesh
from jax.sharding import PartitionSpec as P

WIDTH = 1024
BLOCK = 128
COUNT = WIDTH // BLOCK
PAIRS = COUNT * (COUNT + 1) // 2
HALF = PAIRS // 2
HALF_ROWS = HALF * BLOCK
BASE = 32
AXES = ("y_high", "y_low", "x", "z_high", "z_low", "core")


def qdwh_weights(lower_bound):
    value = lower_bound[0]
    square = value * value
    delta = jnp.cbrt(4.0 * (1.0 - square) / (square * square))
    root = jnp.sqrt(1.0 + delta)
    alpha = root + 0.5 * jnp.sqrt(8.0 - 4.0 * delta + 8.0 * (2.0 - square) / (square * root))
    beta = (alpha - 1.0) ** 2 / 4.0
    shift = alpha + beta - 1.0
    return (beta / shift, alpha - beta / shift, shift)


def iota(shape, dimension):
    return lax.broadcasted_iota(jnp.int32, shape, dimension)


def dot_nn(left, right):
    return jnp.dot(left, right, preferred_element_type=jnp.float32)


def dot_nt(left, right):
    return lax.dot_general(
        left, right, (((1,), (1,)), ((), ())), preferred_element_type=jnp.float32
    )


def dot_tn(left, right):
    return lax.dot_general(
        left, right, (((0,), (0,)), ((), ())), preferred_element_type=jnp.float32
    )


def split(value):
    high = value.astype(jnp.bfloat16)
    rest = value - high.astype(jnp.float32)
    middle = rest.astype(jnp.bfloat16)
    low = (rest - middle.astype(jnp.float32)).astype(jnp.bfloat16)
    return high, middle, low


def left_terms(value, axis):
    high, middle, low = split(value)
    return jnp.concatenate([high, high, middle, high, low, middle], axis=axis)


def right_terms(value, axis):
    high, middle, low = split(value)
    return jnp.concatenate([high, middle, high, low, high, middle], axis=axis)


def block_pairs():
    return [(row, column) for row in range(COUNT) for column in range(row, COUNT)]


def gram_kernel(slab_ref, mine_ref, other_ref):
    core = lax.axis_index("core")
    for side in range(2):

        @pl.when(core == side)
        def _():
            position = 0
            for row in range(COUNT):
                product = dot_tn(
                    slab_ref[:, row * BLOCK : (row + 1) * BLOCK], slab_ref[:, row * BLOCK :]
                )
                for step in range(COUNT - row):
                    half, place = divmod(position, HALF)
                    target = mine_ref if half == side else other_ref
                    target[place * BLOCK : (place + 1) * BLOCK, :] = product[
                        :, step * BLOCK : (step + 1) * BLOCK
                    ]
                    position += 1


def gram_blocks(slab):
    shape = jax.ShapeDtypeStruct((HALF_ROWS, BLOCK), jnp.float32)
    return pl.pallas_call(
        gram_kernel,
        out_shape=(shape, shape),
        in_specs=[pl.BlockSpec(memory_space=pltpu.VMEM)],
        out_specs=(pl.BlockSpec(memory_space=pltpu.VMEM),) * 2,
        compiler_params=pltpu.CompilerParams(vmem_limit_bytes=32 * 2**20),
    )(slab)


def eliminate(row, offset):
    groups = BASE // 8
    lane = iota((8, BLOCK), 1)
    sub = iota((8, BLOCK), 0)
    columns = []
    for column in range(BASE):
        columns.append(
            [
                None
                if group < column // 8
                else jnp.broadcast_to(
                    row[8 * group : 8 * group + 8, offset + column : offset + column + 1],
                    (8, BLOCK),
                )
                for group in range(groups)
            ]
        )
    result = []
    for group in range(groups):
        eye = jnp.where(lane == sub + (offset + 8 * group), 1.0, 0.0)
        inside = (lane >= offset) & (lane < offset + BASE)
        result.append(jnp.where(inside, eye, row[8 * group : 8 * group + 8]))
    pivots = [jnp.ones((8, BLOCK), jnp.float32) for _ in range(groups)]

    def spread(value, sublane):
        return jnp.broadcast_to(value[sublane : sublane + 1], (8, BLOCK))

    for column in range(BASE):
        home, sublane = divmod(column, 8)
        current = columns[column]
        pivot = spread(current[home], sublane)
        inverse_pivot = 1.0 / pivot
        pivots[home] = jnp.where(sub == sublane, pivot, pivots[home])
        scaled = [None] * groups
        for group in range(home, groups):
            scaled[group] = current[group] * inverse_pivot
        for later in range(column + 1, BASE):
            factor = spread(current[later // 8], later % 8)
            for group in range(later // 8, groups):
                columns[later][group] = columns[later][group] - scaled[group] * factor
        source = spread(result[home], sublane)
        for group in range(home, groups):
            multiplier = scaled[group]
            if group == home:
                if sublane == 7:
                    continue
                multiplier = jnp.where(sub > sublane, multiplier, 0.0)
            result[group] = result[group] - multiplier * source
    return jnp.concatenate(
        [result[group] * lax.rsqrt(pivots[group]) for group in range(groups)], axis=0
    )


def inverse_factor_block(block):
    count = BLOCK // BASE
    rows = [block[BASE * index : BASE * (index + 1)] for index in range(count)]
    lane = iota((BASE, BLOCK), 1)
    out = []
    for index in range(count):
        start = BASE * index
        done = eliminate(rows[index], start)
        out.append(jnp.where(lane < start + BASE, done, 0.0))
        if index + 1 < count:
            update = dot_tn(left_terms(done, 0), right_terms(done, 0))
            for later in range(index + 1, count):
                kept = jnp.where((lane >= start) & (lane < start + BASE), 0.0, rows[later])
                rows[later] = kept - update[BASE * later : BASE * (later + 1)]
    return jnp.concatenate(out, axis=0)


def step_kernel(
    weights_ref, mine_ref, other_ref, slab_ref, out_ref, check_ref,
    matrix, panel, terms, solved, checksum, checked,
):
    core = lax.axis_index("core")
    first, second, scale = weights_ref[0], weights_ref[1], weights_ref[2]
    diagonal = jnp.where(iota((BLOCK, BLOCK), 0) == iota((BLOCK, BLOCK), 1), 1.0, 0.0)
    matrix[...] = jnp.zeros_like(matrix)
    for side in range(2):

        @pl.when(core == side)
        def _():
            for position, (row, column) in enumerate(block_pairs()):
                half, place = divmod(position, HALF)
                source = mine_ref if half == side else other_ref
                value = source[place * BLOCK : (place + 1) * BLOCK, :] * scale
                if row == column:
                    value = value + diagonal
                matrix[
                    row * BLOCK : (row + 1) * BLOCK, column * BLOCK : (column + 1) * BLOCK
                ] = value

    column_block = iota((BLOCK, WIDTH), 1) // BLOCK
    rows_dev = slab_ref.shape[0]
    checksum[...] = jnp.broadcast_to(
        jnp.sum(slab_ref[...].astype(jnp.float32), axis=0, keepdims=True) / (rows_dev**0.5),
        checksum.shape,
    )
    checked[...] = jnp.zeros_like(checked)
    solved[...] = jnp.zeros_like(solved)

    def step(index, carry):
        here = pl.ds(pl.multiple_of(index * BLOCK, BLOCK), BLOCK)
        inverse_block = inverse_factor_block(matrix[here, here])
        panel[...] = dot_nn(left_terms(inverse_block, 1), right_terms(matrix[here, :], 0))
        panel[:, here] = inverse_block
        value = panel[...]
        terms[...] = right_terms(value, 0)

        def update(later, carry):
            there = pl.ds(pl.multiple_of(later * BLOCK, BLOCK), BLOCK)
            left = left_terms(panel[:, there].T, 1)
            kept = jnp.where(column_block == index, 0.0, matrix[there, :])
            matrix[there, :] = kept - dot_nn(left, terms[...])
            return carry

        lax.fori_loop(index + 1, COUNT, update, 0)
        inverse = jnp.where(column_block <= index, value, 0.0)
        inverse_half = inverse.astype(jnp.bfloat16)
        projected = dot_nt(slab_ref[...], inverse_half).astype(jnp.bfloat16)
        solved[...] += dot_nn(projected, inverse_half)
        weight = jnp.sum(inverse * checksum[0:1, :], axis=1, keepdims=True)
        checked[...] += (inverse * weight).reshape(BLOCK // 8, 8, WIDTH).sum(axis=0)
        return carry

    lax.fori_loop(0, COUNT, step, 0)
    out_ref[...] = first * slab_ref[...].astype(jnp.float32) + second * solved[...]
    check_ref[...] = first * checksum[0:1, :] + second * jnp.sum(
        checked[...], axis=0, keepdims=True
    )


def polar_step(weights, mine, other, slab):
    rows_dev = slab.shape[0]
    vmem = pl.BlockSpec(memory_space=pltpu.VMEM)
    return pl.pallas_call(
        step_kernel,
        out_shape=(
            jax.ShapeDtypeStruct((rows_dev, WIDTH), jnp.float32),
            jax.ShapeDtypeStruct((1, WIDTH), jnp.float32),
        ),
        in_specs=[pl.BlockSpec(memory_space=pltpu.SMEM), vmem, vmem, vmem],
        out_specs=(vmem, vmem),
        scratch_shapes=[
            pltpu.VMEM((WIDTH, WIDTH), jnp.float32),
            pltpu.VMEM((BLOCK, WIDTH), jnp.float32),
            pltpu.VMEM((6 * BLOCK, WIDTH), jnp.bfloat16),
            pltpu.VMEM((rows_dev, WIDTH), jnp.float32),
            pltpu.VMEM((8, WIDTH), jnp.float32),
            pltpu.VMEM((8, WIDTH), jnp.float32),
        ],
        compiler_params=pltpu.CompilerParams(vmem_limit_bytes=48 * 2**20),
    )(weights, mine, other, slab)


def exchange(parts, axis):
    return lax.all_to_all(parts, axis, 0, 0, tiled=True)


def shared(part, count):
    return jnp.broadcast_to(part[None], (count,) + part.shape)


def swap(value):
    return lax.ppermute(value, "core", [(0, 1), (1, 0)])


def sum_over_devices(mine, other):
    near = ("x", "y_low", "z_low")
    count = 1
    for name in near:
        count *= lax.axis_size(name)
    own = mine + swap(other)
    own = exchange(own.reshape(count, -1, BLOCK), near).sum(axis=0)
    for name in ("y_high", "z_high"):
        own = exchange(shared(own, lax.axis_size(name)), name).sum(axis=0)
    own = exchange(shared(own, count), near).reshape(-1, BLOCK)
    return own, swap(own)


def per_device(slab, lower_bound):
    devices_all = 1
    for name in AXES:
        devices_all *= lax.axis_size(name)
    first, second, shift = qdwh_weights(lower_bound)
    weights = jnp.stack([first, second, shift / (slab.shape[0] * devices_all)])
    mine, other = sum_over_devices(*gram_blocks(slab))
    return polar_step(weights, mine, other, slab)


def solution(mesh):
    wide = Mesh(mesh.devices.reshape(4, 2, 4, 4, 2, 2), AXES)
    return jax.shard_map(
        per_device,
        mesh=wide,
        in_specs=(P(AXES, None), P()),
        out_specs=(P(AXES, None), P(AXES, None)),
        check_vma=False,
    )
```

```python
import jax
import jax.numpy as jnp
from jax import lax
from jax.experimental import pallas as pl
from jax.experimental.pallas import tpu as pltpu
from jax.sharding import Mesh
from jax.sharding import PartitionSpec as P

WIDTH = 1024
BLOCK = 128
COUNT = WIDTH // BLOCK
PAIRS = COUNT * (COUNT + 1) // 2
HALF = PAIRS // 2
HALF_ROWS = HALF * BLOCK
BASE = 64
GROUP = 8
AHEAD = 3
AXES = ("y_high", "y_low", "x", "z_high", "z_low", "core")


def qdwh_weights(lower_bound):
    value = lower_bound[0]
    square = value * value
    delta = jnp.cbrt(4.0 * (1.0 - square) / (square * square))
    root = jnp.sqrt(1.0 + delta)
    alpha = root + 0.5 * jnp.sqrt(8.0 - 4.0 * delta + 8.0 * (2.0 - square) / (square * root))
    beta = (alpha - 1.0) ** 2 / 4.0
    shift = alpha + beta - 1.0
    return (beta / shift, alpha - beta / shift, shift)


def iota(shape, dimension):
    return lax.broadcasted_iota(jnp.int32, shape, dimension)


def dot_nn(left, right):
    return jnp.dot(left, right, preferred_element_type=jnp.float32)


def dot_nt(left, right):
    return lax.dot_general(
        left, right, (((1,), (1,)), ((), ())), preferred_element_type=jnp.float32
    )


def dot_tn(left, right):
    return lax.dot_general(
        left, right, (((0,), (0,)), ((), ())), preferred_element_type=jnp.float32
    )


def split(value):
    high = value.astype(jnp.bfloat16)
    rest = value - high.astype(jnp.float32)
    middle = rest.astype(jnp.bfloat16)
    low = (rest - middle.astype(jnp.float32)).astype(jnp.bfloat16)
    return high, middle, low


def left_terms(parts, axis):
    high, middle, low = parts
    return jnp.concatenate([high, high, middle, high, low, middle], axis=axis)


def right_terms(parts, axis):
    high, middle, low = parts
    return jnp.concatenate([high, middle, high, low, high, middle], axis=axis)


def block_pairs():
    return [(row, column) for row in range(COUNT) for column in range(row, COUNT)]


def gram_kernel(slab_ref, mine_ref, other_ref):
    core = lax.axis_index("core")
    for side in range(2):

        @pl.when(core == side)
        def _():
            position = 0
            for row in range(COUNT):
                product = dot_tn(
                    slab_ref[:, row * BLOCK : (row + 1) * BLOCK], slab_ref[:, row * BLOCK :]
                )
                for step in range(COUNT - row):
                    half, place = divmod(position, HALF)
                    target = mine_ref if half == side else other_ref
                    target[place * BLOCK : (place + 1) * BLOCK, :] = product[
                        :, step * BLOCK : (step + 1) * BLOCK
                    ]
                    position += 1


def gram_blocks(slab):
    shape = jax.ShapeDtypeStruct((HALF_ROWS, BLOCK), jnp.float32)
    return pl.pallas_call(
        gram_kernel,
        out_shape=(shape, shape),
        in_specs=[pl.BlockSpec(memory_space=pltpu.VMEM)],
        out_specs=(pl.BlockSpec(memory_space=pltpu.VMEM),) * 2,
        compiler_params=pltpu.CompilerParams(vmem_limit_bytes=32 * 2**20),
    )(slab)


def spread(value, sublane):
    return jnp.broadcast_to(value[sublane : sublane + 1], (8, BLOCK))


def eliminate(row, offset, out):
    groups = BASE // 8
    lane = iota((8, BLOCK), 1)
    sub = iota((8, BLOCK), 0)
    result = [row[8 * group : 8 * group + 8] for group in range(groups)]

    def copied(start):
        return {
            column: [
                None
                if group < column // 8
                else jnp.broadcast_to(
                    result[group][:, offset + column : offset + column + 1], (8, BLOCK)
                )
                for group in range(groups)
            ]
            for column in range(start, start + GROUP)
        }

    pivots = [jnp.ones((8, BLOCK), jnp.float32) for _ in range(groups)]
    columns = copied(0)
    for column in range(BASE):
        home, sublane = divmod(column, 8)
        current = columns.pop(column)
        pivot = spread(current[home], sublane)
        inverse_pivot = 1.0 / pivot
        pivots[home] = jnp.where(sub == sublane, pivot, pivots[home])
        scaled = {group: current[group] * inverse_pivot for group in range(home, groups)}
        for later, values in columns.items():
            factor = spread(current[later // 8], later % 8)
            for group in range(later // 8, groups):
                values[group] = values[group] - scaled[group] * factor
        here = lane == offset + column
        source = jnp.where(here, 1.0, spread(result[home], sublane))
        for group in range(home, groups):
            if group == home:
                kept = jnp.where(here, jnp.where(sub == sublane, 1.0, 0.0), result[group])
                if sublane < 7:
                    kept = kept - jnp.where(sub > sublane, scaled[group], 0.0) * source
                result[group] = kept
            else:
                kept = jnp.where(here, 0.0, result[group])
                result[group] = kept - scaled[group] * source
        if column % GROUP == AHEAD and column - AHEAD + GROUP < BASE:
            columns.update(copied(column - AHEAD + GROUP))
        yield
    for group in range(groups):
        upper = (lane > sub + (offset + 8 * group)) & (lane < offset + BASE)
        kept = jnp.where(upper, 0.0, result[group])
        out.append(kept * lax.rsqrt(pivots[group]))


def factor_block(block, beside, beyond, out):
    count = BLOCK // BASE
    rows = [block[BASE * index : BASE * (index + 1)] for index in range(count)]
    lane = iota((BASE, BLOCK), 1)
    inverse, panel, following = [], [], None
    for index in range(count):
        done = []
        yield from eliminate(rows[index], BASE * index, done)
        done = jnp.concatenate(done, axis=0)
        start, stop = BASE * index, BASE * (index + 1)
        if index + 1 < count:
            parts = split(done)
            change = dot_tn(left_terms(parts, 0), right_terms(parts, 0))
            for later in range(index + 1, count):
                kept = jnp.where((lane >= start) & (lane < stop), 0.0, rows[later])
                rows[later] = kept - change[BASE * later : BASE * (later + 1)]
        inverse.append(jnp.where(lane < stop, done, 0.0))
        if beside is not None:
            if index == 0:
                source, following = beside(), beyond()
            piece = dot_nn(
                left_terms(split(inverse[-1][:, :stop]), 1), right_terms(split(source[:stop]), 0)
            )
            parts = split(piece)
            following = following - dot_tn(left_terms(parts, 0), right_terms(parts, 0))
            panel.append(piece)
        yield
    out.append(jnp.concatenate(inverse, axis=0))
    out.append(jnp.concatenate(panel, axis=0) if panel else None)
    out.append(following)


def weave(steps, tasks):
    count = (BLOCK // BASE) * (BASE + 1)
    done = 0
    for place, _ in enumerate(steps):
        while done < len(tasks) and done * count < (place + 1) * len(tasks):
            tasks[done]()
            done += 1
    while done < len(tasks):
        tasks[done]()
        done += 1


def block_slice(start, stop=None):
    return slice(BLOCK * start, BLOCK * (start + 1 if stop is None else stop))


def step_kernel(
    weights_ref, mine_ref, other_ref, slab_ref, out_ref, check_ref,
    matrix, panel, panel_parts, left_parts, solved, checksum, checked,
):
    low_core = lax.axis_index("core") == 0
    first, second, scale = weights_ref[0], weights_ref[1], weights_ref[2]
    identity = jnp.where(iota((BLOCK, BLOCK), 0) == iota((BLOCK, BLOCK), 1), 1.0, 0.0)
    places = {pair: divmod(place, HALF) for place, pair in enumerate(block_pairs())}
    rows_dev = slab_ref.shape[0]

    def load(row, column):
        half, place = places[row, column]
        here = block_slice(place)
        value = jnp.where(low_core == (half == 0), mine_ref[here, :], other_ref[here, :]) * scale
        matrix[block_slice(row), block_slice(column)] = value + identity if row == column else value

    def sum_rows(start, stop):
        here = block_slice(start, stop)
        total = jnp.sum(slab_ref[:, here].astype(jnp.float32), axis=0, keepdims=True)
        checksum[:, here] = total / (rows_dev**0.5)

    def keep_panel(start, value):
        here = slice(BLOCK * start, BLOCK * start + value.shape[1])
        panel[:, here] = value
        for index, part in enumerate(split(value)):
            panel_parts[block_slice(index), here] = part

    def make_panel(index, inverse_parts, start, stop):
        source = right_terms(split(matrix[block_slice(index), block_slice(start, stop)]), 0)
        keep_panel(start, dot_nn(inverse_parts, source))

    def turn_panel(row):
        for index, part in enumerate(split(panel[:, block_slice(row)].T)):
            left_parts[block_slice(row), block_slice(index)] = part

    def product(row, row_stop, start, stop):
        rows, columns = block_slice(row, row_stop), block_slice(start, stop)
        left = left_terms([left_parts[rows, block_slice(index)] for index in range(3)], 1)
        right = right_terms([panel_parts[block_slice(index), columns] for index in range(3)], 0)
        return dot_nn(left, right)

    def update_right(index, start, stop):
        rows, columns = block_slice(index + 1, stop), block_slice(start, stop)
        matrix[rows, columns] = matrix[rows, columns] - product(index + 1, stop, start, stop)

    def update_left(index, start, stop):
        change = product(index + 1, COUNT, start, stop)
        rows = block_slice(index + 1, COUNT)
        known = min(stop, index)
        width = BLOCK * (known - start)
        if known > start:
            columns = block_slice(start, known)
            matrix[rows, columns] = matrix[rows, columns] - change[:, :width]
        if stop > index:
            matrix[rows, block_slice(index)] = -change[:, width:]

    def project(index, held):
        columns = block_slice(0, index + 1)
        held.append(
            dot_nt(slab_ref[:, columns], panel_parts[:BLOCK, columns]).astype(jnp.bfloat16)
        )

    def solve(index, held, start, stop):
        columns = block_slice(start, stop)
        value = dot_nn(held[0], panel_parts[:BLOCK, columns])
        width = BLOCK * (min(stop, index) - start)
        if width > 0:
            known = solved[:, BLOCK * start : BLOCK * start + width] + value[:, :width]
            value = jnp.concatenate([known, value[:, width:]], axis=1) if stop > index else known
        if index + 1 == COUNT:
            out_ref[:, columns] = first * slab_ref[:, columns].astype(jnp.float32) + second * value
        else:
            solved[:, columns] = value

    def check(index):
        columns = block_slice(0, index + 1)
        inverse = panel[:, columns]
        weight = jnp.sum(inverse * checksum[:, columns], axis=1, keepdims=True)
        change = (inverse * weight).reshape(BLOCK // 8, 8, inverse.shape[1]).sum(axis=0)
        if index:
            known = block_slice(0, index)
            checked[:, known] = checked[:, known] + change[:, : BLOCK * index]
        checked[:, block_slice(index)] = change[:, BLOCK * index :]

    tasks = []

    def later(function, *arguments):
        tasks.append(lambda: function(*arguments))

    load(0, 0)
    for pair in places:
        if pair != (0, 0):
            later(load, *pair)
    for start in range(0, COUNT, 2):
        later(sum_rows, start, start + 2)
    diagonal = matrix[block_slice(0), block_slice(0)]
    for index in range(COUNT):
        beside = beyond = None
        if index + 1 < COUNT:
            beside = lambda at=index: matrix[block_slice(at), block_slice(at + 1)]
            beyond = lambda at=index: matrix[block_slice(at + 1), block_slice(at + 1)]
        found = []
        weave(factor_block(diagonal, beside, beyond, found), tasks)
        inverse, neighbour, diagonal = found
        inverse_parts = left_terms(split(inverse), 1)
        tasks = []
        keep_panel(index, inverse)
        if neighbour is not None:
            keep_panel(index + 1, neighbour)
            later(turn_panel, index + 1)
            start = index + 2
            while start < COUNT:
                stop = start + 2 - start % 2
                later(make_panel, index, inverse_parts, start, stop)
                for row in range(start, stop):
                    later(turn_panel, row)
                later(update_right, index, start, stop)
                start = stop
        for start in range(0, index, 2):
            later(make_panel, index, inverse_parts, start, min(start + 2, index))
        if index + 1 < COUNT:
            for start in range(0, index + 1, 2):
                later(update_left, index, start, min(start + 2, index + 1))
        held = []
        later(project, index, held)
        for start in range(0, index + 1, 2):
            later(solve, index, held, start, min(start + 2, index + 1))
        later(check, index)
    for task in tasks:
        task()
    check_ref[...] = first * checksum[...] + second * jnp.sum(checked[...], axis=0, keepdims=True)


def polar_step(weights, mine, other, slab):
    rows_dev = slab.shape[0]
    vmem = pl.BlockSpec(memory_space=pltpu.VMEM)
    return pl.pallas_call(
        step_kernel,
        out_shape=(
            jax.ShapeDtypeStruct((rows_dev, WIDTH), jnp.float32),
            jax.ShapeDtypeStruct((1, WIDTH), jnp.float32),
        ),
        in_specs=[pl.BlockSpec(memory_space=pltpu.SMEM), vmem, vmem, vmem],
        out_specs=(vmem, vmem),
        scratch_shapes=[
            pltpu.VMEM((WIDTH, WIDTH), jnp.float32),
            pltpu.VMEM((BLOCK, WIDTH), jnp.float32),
            pltpu.VMEM((3 * BLOCK, WIDTH), jnp.bfloat16),
            pltpu.VMEM((WIDTH, 3 * BLOCK), jnp.bfloat16),
            pltpu.VMEM((rows_dev, WIDTH), jnp.float32),
            pltpu.VMEM((1, WIDTH), jnp.float32),
            pltpu.VMEM((8, WIDTH), jnp.float32),
        ],
        compiler_params=pltpu.CompilerParams(vmem_limit_bytes=48 * 2**20),
    )(weights, mine, other, slab)


def exchange(parts, axis):
    return lax.all_to_all(parts, axis, 0, 0, tiled=True)


def shared(part, count):
    return jnp.broadcast_to(part[None], (count,) + part.shape)


def swap(value):
    return lax.ppermute(value, "core", [(0, 1), (1, 0)])


def sum_over_devices(mine, other):
    near = ("x", "y_low", "z_low")
    count = 1
    for name in near:
        count *= lax.axis_size(name)
    own = mine + swap(other)
    own = exchange(own.reshape(count, -1, BLOCK), near).sum(axis=0)
    for name in ("y_high", "z_high"):
        own = exchange(shared(own, lax.axis_size(name)), name).sum(axis=0)
    own = exchange(shared(own, count), near).reshape(-1, BLOCK)
    return own, swap(own)


def per_device(slab, lower_bound):
    devices_all = 1
    for name in AXES:
        devices_all *= lax.axis_size(name)
    first, second, shift = qdwh_weights(lower_bound)
    weights = jnp.stack([first, second, shift / (slab.shape[0] * devices_all)])
    mine, other = sum_over_devices(*gram_blocks(slab))
    return polar_step(weights, mine, other, slab)


def solution(mesh):
    wide = Mesh(mesh.devices.reshape(4, 2, 4, 4, 2, 2), AXES)
    return jax.shard_map(
        per_device,
        mesh=wide,
        in_specs=(P(AXES, None), P()),
        out_specs=(P(AXES, None), P(AXES, None)),
        check_vma=False,
    )
```

```python
import jax
import jax.numpy as jnp
from jax import lax
from jax.experimental import pallas as pl
from jax.experimental.pallas import tpu as pltpu
from jax.sharding import Mesh
from jax.sharding import PartitionSpec as P

WIDTH = 1024
BLOCK = 128
COUNT = WIDTH // BLOCK
HALF = (COUNT * (COUNT - 1) // 2 + COUNT // 2 + 2) // 2
HALF_ROWS = HALF * BLOCK
BASE = 64
GROUP = 8
AHEAD = 3
AXES = ("y_high", "y_low", "x", "z_high", "z_low", "core")


def qdwh_weights(lower_bound):
    value = lower_bound[0]
    square = value * value
    delta = jnp.cbrt(4.0 * (1.0 - square) / (square * square))
    root = jnp.sqrt(1.0 + delta)
    alpha = root + 0.5 * jnp.sqrt(8.0 - 4.0 * delta + 8.0 * (2.0 - square) / (square * root))
    beta = (alpha - 1.0) ** 2 / 4.0
    shift = alpha + beta - 1.0
    return (beta / shift, alpha - beta / shift, shift)


def iota(shape, dimension):
    return lax.broadcasted_iota(jnp.int32, shape, dimension)


def dot_nn(left, right):
    return jnp.dot(left, right, preferred_element_type=jnp.float32)


def dot_nt(left, right):
    return lax.dot_general(
        left, right, (((1,), (1,)), ((), ())), preferred_element_type=jnp.float32
    )


def dot_tn(left, right):
    return lax.dot_general(
        left, right, (((0,), (0,)), ((), ())), preferred_element_type=jnp.float32
    )


def split(value):
    high = value.astype(jnp.bfloat16)
    rest = value - high.astype(jnp.float32)
    middle = rest.astype(jnp.bfloat16)
    low = (rest - middle.astype(jnp.float32)).astype(jnp.bfloat16)
    return high, middle, low


def left_terms(parts, axis):
    high, middle, low = parts
    return jnp.concatenate([high, high, middle, high, low, middle], axis=axis)


def right_terms(parts, axis):
    high, middle, low = parts
    return jnp.concatenate([high, middle, high, low, high, middle], axis=axis)


def block_places():
    names = [(row, column) for row in range(COUNT) for column in range(row + 1, COUNT)]
    names += [(row, row) for row in range(0, COUNT, 2)] + ["diagonals", "unused"]
    return {name: divmod(place, HALF) for place, name in enumerate(names)}


def gram_kernel(slab_ref, mine_ref, other_ref):
    core = lax.axis_index("core")
    across, down = iota((BLOCK, BLOCK), 1), iota((BLOCK, BLOCK), 0)
    places = block_places()
    for side in range(2):

        @pl.when(core == side)
        def _():
            def keep(name, value):
                half, place = places[name]
                target = mine_ref if half == side else other_ref
                target[place * BLOCK : (place + 1) * BLOCK, :] = value

            even, diagonals = None, []
            for row in range(COUNT):
                product = dot_tn(
                    slab_ref[:, row * BLOCK : (row + 1) * BLOCK], slab_ref[:, row * BLOCK :]
                )
                for column in range(row + 1, COUNT):
                    start = (column - row) * BLOCK
                    keep((row, column), product[:, start : start + BLOCK])
                square = product[:, :BLOCK]
                if row % 2 == 0:
                    even = square
                else:
                    keep((row - 1, row - 1), jnp.where(across >= down, even, square))
                    on_it = jnp.where(across == down, square, 0.0)
                    diagonals.append(jnp.sum(on_it, axis=0, keepdims=True))
            total = jnp.zeros((BLOCK, BLOCK), jnp.float32)
            for index, value in enumerate(diagonals):
                total = jnp.where(down == index, value, total)
            keep("diagonals", total)
            keep("unused", jnp.zeros((BLOCK, BLOCK), jnp.float32))


def gram_blocks(slab):
    shape = jax.ShapeDtypeStruct((HALF_ROWS, BLOCK), jnp.float32)
    return pl.pallas_call(
        gram_kernel,
        out_shape=(shape, shape),
        in_specs=[pl.BlockSpec(memory_space=pltpu.VMEM)],
        out_specs=(pl.BlockSpec(memory_space=pltpu.VMEM),) * 2,
        compiler_params=pltpu.CompilerParams(vmem_limit_bytes=32 * 2**20),
    )(slab)


def spread(value, sublane):
    return jnp.broadcast_to(value[sublane : sublane + 1], (8, BLOCK))


def eliminate(row, offset, out):
    groups = BASE // 8
    lane = iota((8, BLOCK), 1)
    sub = iota((8, BLOCK), 0)
    result = [row[8 * group : 8 * group + 8] for group in range(groups)]

    def copied(start):
        return {
            column: [
                None
                if group < column // 8
                else jnp.broadcast_to(
                    result[group][:, offset + column : offset + column + 1], (8, BLOCK)
                )
                for group in range(groups)
            ]
            for column in range(start, start + GROUP)
        }

    pivots = [jnp.ones((8, BLOCK), jnp.float32) for _ in range(groups)]
    columns = copied(0)
    for column in range(BASE):
        home, sublane = divmod(column, 8)
        current = columns.pop(column)
        pivot = spread(current[home], sublane)
        inverse_pivot = 1.0 / pivot
        pivots[home] = jnp.where(sub == sublane, pivot, pivots[home])
        scaled = {group: current[group] * inverse_pivot for group in range(home, groups)}
        for later, values in columns.items():
            factor = spread(current[later // 8], later % 8)
            for group in range(later // 8, groups):
                values[group] = values[group] - scaled[group] * factor
        here = lane == offset + column
        source = jnp.where(here, 1.0, spread(result[home], sublane))
        for group in range(home, groups):
            if group == home:
                kept = jnp.where(here, jnp.where(sub == sublane, 1.0, 0.0), result[group])
                if sublane < 7:
                    kept = kept - jnp.where(sub > sublane, scaled[group], 0.0) * source
                result[group] = kept
            else:
                kept = jnp.where(here, 0.0, result[group])
                result[group] = kept - scaled[group] * source
        if column % GROUP == AHEAD and column - AHEAD + GROUP < BASE:
            columns.update(copied(column - AHEAD + GROUP))
        yield
    for group in range(groups):
        upper = (lane > sub + (offset + 8 * group)) & (lane < offset + BASE)
        kept = jnp.where(upper, 0.0, result[group])
        out.append(kept * lax.rsqrt(pivots[group]))


def factor_block(block, beside, beyond, out):
    count = BLOCK // BASE
    rows = [block[BASE * index : BASE * (index + 1)] for index in range(count)]
    lane = iota((BASE, BLOCK), 1)
    inverse, panel, following = [], [], None
    for index in range(count):
        done = []
        yield from eliminate(rows[index], BASE * index, done)
        done = jnp.concatenate(done, axis=0)
        start, stop = BASE * index, BASE * (index + 1)
        if index + 1 < count:
            parts = split(done)
            change = dot_tn(left_terms(parts, 0), right_terms(parts, 0))
            for later in range(index + 1, count):
                kept = jnp.where((lane >= start) & (lane < stop), 0.0, rows[later])
                rows[later] = kept - change[BASE * later : BASE * (later + 1)]
        inverse.append(jnp.where(lane < stop, done, 0.0))
        if beside is not None:
            if index == 0:
                source, following = beside(), beyond()
            piece = dot_nn(
                left_terms(split(inverse[-1][:, :stop]), 1), right_terms(split(source[:stop]), 0)
            )
            parts = split(piece)
            following = following - dot_tn(left_terms(parts, 0), right_terms(parts, 0))
            panel.append(piece)
        yield
    out.append(jnp.concatenate(inverse, axis=0))
    out.append(jnp.concatenate(panel, axis=0) if panel else None)
    out.append(following)


def weave(steps, tasks):
    count = (BLOCK // BASE) * (BASE + 1)
    done = 0
    for place, _ in enumerate(steps):
        while done < len(tasks) and done * count < (place + 1) * len(tasks):
            tasks[done]()
            done += 1
    while done < len(tasks):
        tasks[done]()
        done += 1


def block_slice(start, stop=None):
    return slice(BLOCK * start, BLOCK * (start + 1 if stop is None else stop))


def step_kernel(
    weights_ref, mine_ref, other_ref, slab_ref, out_ref, check_ref,
    matrix, panel, panel_parts, left_parts, solved, checksum, checked,
):
    low_core = lax.axis_index("core") == 0
    first, second, scale = weights_ref[0], weights_ref[1], weights_ref[2]
    across, down = iota((BLOCK, BLOCK), 1), iota((BLOCK, BLOCK), 0)
    identity = jnp.where(across == down, 1.0, 0.0)
    places = block_places()
    rows_dev = slab_ref.shape[0]

    def fetch(name, rows=slice(0, BLOCK)):
        half, place = places[name]
        here = slice(place * BLOCK + rows.start, place * BLOCK + rows.stop)
        return jnp.where(low_core == (half == 0), mine_ref[here, :], other_ref[here, :]) * scale

    def load(row, column):
        value = fetch((row, column))
        if row == column:
            turned = value.T
            extra = fetch("diagonals", slice(row // 2, row // 2 + 1))
            odd = jnp.where(across < down, value, jnp.where(across > down, turned, extra))
            value = jnp.where(across >= down, value, turned) + identity
            matrix[block_slice(row + 1), block_slice(row + 1)] = odd + identity
        matrix[block_slice(row), block_slice(column)] = value

    def sum_rows(start, stop):
        here = block_slice(start, stop)
        total = jnp.sum(slab_ref[:, here].astype(jnp.float32), axis=0, keepdims=True)
        checksum[:, here] = total / (rows_dev**0.5)

    def keep_panel(start, value):
        here = slice(BLOCK * start, BLOCK * start + value.shape[1])
        panel[:, here] = value
        for index, part in enumerate(split(value)):
            panel_parts[block_slice(index), here] = part

    def make_panel(index, inverse_parts, start, stop):
        source = right_terms(split(matrix[block_slice(index), block_slice(start, stop)]), 0)
        keep_panel(start, dot_nn(inverse_parts, source))

    def turn_panel(row):
        for index, part in enumerate(split(panel[:, block_slice(row)].T)):
            left_parts[block_slice(row), block_slice(index)] = part

    def product(row, row_stop, start, stop):
        rows, columns = block_slice(row, row_stop), block_slice(start, stop)
        left = left_terms([left_parts[rows, block_slice(index)] for index in range(3)], 1)
        right = right_terms([panel_parts[block_slice(index), columns] for index in range(3)], 0)
        return dot_nn(left, right)

    def update_right(index, start, stop):
        rows, columns = block_slice(index + 1, stop), block_slice(start, stop)
        matrix[rows, columns] = matrix[rows, columns] - product(index + 1, stop, start, stop)

    def update_left(index, start, stop):
        change = product(index + 1, COUNT, start, stop)
        rows = block_slice(index + 1, COUNT)
        known = min(stop, index)
        width = BLOCK * (known - start)
        if known > start:
            columns = block_slice(start, known)
            matrix[rows, columns] = matrix[rows, columns] - change[:, :width]
        if stop > index:
            matrix[rows, block_slice(index)] = -change[:, width:]

    def project(index, held):
        columns = block_slice(0, index + 1)
        held.append(
            dot_nt(slab_ref[:, columns], panel_parts[:BLOCK, columns]).astype(jnp.bfloat16)
        )

    def solve(index, held, start, stop):
        columns = block_slice(start, stop)
        value = dot_nn(held[0], panel_parts[:BLOCK, columns])
        width = BLOCK * (min(stop, index) - start)
        if width > 0:
            known = solved[:, BLOCK * start : BLOCK * start + width] + value[:, :width]
            value = jnp.concatenate([known, value[:, width:]], axis=1) if stop > index else known
        if index + 1 == COUNT:
            out_ref[:, columns] = first * slab_ref[:, columns].astype(jnp.float32) + second * value
        else:
            solved[:, columns] = value

    def check(index):
        columns = block_slice(0, index + 1)
        inverse = panel[:, columns]
        weight = jnp.sum(inverse * checksum[:, columns], axis=1, keepdims=True)
        change = (inverse * weight).reshape(BLOCK // 8, 8, inverse.shape[1]).sum(axis=0)
        if index:
            known = block_slice(0, index)
            checked[:, known] = checked[:, known] + change[:, : BLOCK * index]
        checked[:, block_slice(index)] = change[:, BLOCK * index :]

    tasks = []

    def later(function, *arguments):
        tasks.append(lambda: function(*arguments))

    load(0, 0)
    pairs = [name for name in places if isinstance(name, tuple) and name != (0, 0)]
    for pair in sorted(pairs):
        later(load, *pair)
    for start in range(0, COUNT, 2):
        later(sum_rows, start, start + 2)
    diagonal = matrix[block_slice(0), block_slice(0)]
    for index in range(COUNT):
        beside = beyond = None
        if index + 1 < COUNT:
            beside = lambda at=index: matrix[block_slice(at), block_slice(at + 1)]
            beyond = lambda at=index: matrix[block_slice(at + 1), block_slice(at + 1)]
        found = []
        weave(factor_block(diagonal, beside, beyond, found), tasks)
        inverse, neighbour, diagonal = found
        inverse_parts = left_terms(split(inverse), 1)
        tasks = []
        keep_panel(index, inverse)
        if neighbour is not None:
            keep_panel(index + 1, neighbour)
            later(turn_panel, index + 1)
            start = index + 2
            while start < COUNT:
                stop = start + 2 - start % 2
                later(make_panel, index, inverse_parts, start, stop)
                for row in range(start, stop):
                    later(turn_panel, row)
                later(update_right, index, start, stop)
                start = stop
        for start in range(0, index, 2):
            later(make_panel, index, inverse_parts, start, min(start + 2, index))
        if index + 1 < COUNT:
            for start in range(0, index + 1, 2):
                later(update_left, index, start, min(start + 2, index + 1))
        held = []
        later(project, index, held)
        for start in range(0, index + 1, 2):
            later(solve, index, held, start, min(start + 2, index + 1))
        later(check, index)
    for task in tasks:
        task()
    check_ref[...] = first * checksum[...] + second * jnp.sum(checked[...], axis=0, keepdims=True)


def polar_step(weights, mine, other, slab):
    rows_dev = slab.shape[0]
    vmem = pl.BlockSpec(memory_space=pltpu.VMEM)
    return pl.pallas_call(
        step_kernel,
        out_shape=(
            jax.ShapeDtypeStruct((rows_dev, WIDTH), jnp.float32),
            jax.ShapeDtypeStruct((1, WIDTH), jnp.float32),
        ),
        in_specs=[pl.BlockSpec(memory_space=pltpu.SMEM), vmem, vmem, vmem],
        out_specs=(vmem, vmem),
        scratch_shapes=[
            pltpu.VMEM((WIDTH, WIDTH), jnp.float32),
            pltpu.VMEM((BLOCK, WIDTH), jnp.float32),
            pltpu.VMEM((3 * BLOCK, WIDTH), jnp.bfloat16),
            pltpu.VMEM((WIDTH, 3 * BLOCK), jnp.bfloat16),
            pltpu.VMEM((rows_dev, WIDTH), jnp.float32),
            pltpu.VMEM((1, WIDTH), jnp.float32),
            pltpu.VMEM((8, WIDTH), jnp.float32),
        ],
        compiler_params=pltpu.CompilerParams(vmem_limit_bytes=48 * 2**20),
    )(weights, mine, other, slab)


def exchange(parts, axis):
    return lax.all_to_all(parts, axis, 0, 0, tiled=True)


def shared(part, count):
    return jnp.broadcast_to(part[None], (count,) + part.shape)


def swap(value):
    return lax.ppermute(value, "core", [(0, 1), (1, 0)])


def sum_over_devices(mine, other):
    near = ("x", "y_low", "z_low")
    count = 1
    for name in near:
        count *= lax.axis_size(name)
    own = mine + swap(other)
    own = exchange(own.reshape(count, -1, BLOCK), near).sum(axis=0)
    for name in ("y_high", "z_high"):
        own = exchange(shared(own, lax.axis_size(name)), name).sum(axis=0)
    own = exchange(shared(own, count), near).reshape(-1, BLOCK)
    return own, swap(own)


def per_device(slab, lower_bound):
    devices_all = 1
    for name in AXES:
        devices_all *= lax.axis_size(name)
    first, second, shift = qdwh_weights(lower_bound)
    weights = jnp.stack([first, second, shift / (slab.shape[0] * devices_all)])
    mine, other = sum_over_devices(*gram_blocks(slab))
    return polar_step(weights, mine, other, slab)


def solution(mesh):
    wide = Mesh(mesh.devices.reshape(4, 2, 4, 4, 2, 2), AXES)
    return jax.shard_map(
        per_device,
        mesh=wide,
        in_specs=(P(AXES, None), P()),
        out_specs=(P(AXES, None), P(AXES, None)),
        check_vma=False,
    )
```

```python
import jax
import jax.numpy as jnp
from jax import lax
from jax.experimental import pallas as pl
from jax.experimental.pallas import tpu as pltpu
from jax.sharding import Mesh
from jax.sharding import PartitionSpec as P

WIDTH = 1024
BLOCK = 128
COUNT = WIDTH // BLOCK
HALF = (COUNT * (COUNT - 1) // 2 + COUNT // 2 + 2) // 2
HALF_ROWS = HALF * BLOCK
BASE = 64
GROUP = 8
AHEAD = 3
LATER = 36
FOLLOW = 2
AXES = ("y_high", "y_low", "x", "z_high", "z_low", "core")


def qdwh_weights(lower_bound):
    value = lower_bound[0]
    square = value * value
    delta = jnp.cbrt(4.0 * (1.0 - square) / (square * square))
    root = jnp.sqrt(1.0 + delta)
    alpha = root + 0.5 * jnp.sqrt(8.0 - 4.0 * delta + 8.0 * (2.0 - square) / (square * root))
    beta = (alpha - 1.0) ** 2 / 4.0
    shift = alpha + beta - 1.0
    return (beta / shift, alpha - beta / shift, shift)


def iota(shape, dimension):
    return lax.broadcasted_iota(jnp.int32, shape, dimension)


def dot_nn(left, right):
    return jnp.dot(left, right, preferred_element_type=jnp.float32)


def dot_nt(left, right):
    return lax.dot_general(
        left, right, (((1,), (1,)), ((), ())), preferred_element_type=jnp.float32
    )


def dot_tn(left, right):
    return lax.dot_general(
        left, right, (((0,), (0,)), ((), ())), preferred_element_type=jnp.float32
    )


def split(value):
    high = value.astype(jnp.bfloat16)
    rest = value - high.astype(jnp.float32)
    middle = rest.astype(jnp.bfloat16)
    low = (rest - middle.astype(jnp.float32)).astype(jnp.bfloat16)
    return high, middle, low


def left_terms(parts, axis):
    high, middle, low = parts
    return jnp.concatenate([high, high, middle, high, low, middle], axis=axis)


def right_terms(parts, axis):
    high, middle, low = parts
    return jnp.concatenate([high, middle, high, low, high, middle], axis=axis)


def block_places():
    names = [(row, column) for row in range(COUNT) for column in range(row + 1, COUNT)]
    names += [(row, row) for row in range(0, COUNT, 2)] + ["diagonals", "unused"]
    return {name: divmod(place, HALF) for place, name in enumerate(names)}


def gram_kernel(slab_ref, mine_ref, other_ref):
    core = lax.axis_index("core")
    across, down = iota((BLOCK, BLOCK), 1), iota((BLOCK, BLOCK), 0)
    places = block_places()
    for side in range(2):

        @pl.when(core == side)
        def _():
            def keep(name, value):
                half, place = places[name]
                target = mine_ref if half == side else other_ref
                target[place * BLOCK : (place + 1) * BLOCK, :] = value

            even, diagonals = None, []
            for row in range(COUNT):
                product = dot_tn(
                    slab_ref[:, row * BLOCK : (row + 1) * BLOCK], slab_ref[:, row * BLOCK :]
                )
                for column in range(row + 1, COUNT):
                    start = (column - row) * BLOCK
                    keep((row, column), product[:, start : start + BLOCK])
                square = product[:, :BLOCK]
                if row % 2 == 0:
                    even = square
                else:
                    keep((row - 1, row - 1), jnp.where(across >= down, even, square))
                    on_it = jnp.where(across == down, square, 0.0)
                    diagonals.append(jnp.sum(on_it, axis=0, keepdims=True))
            total = jnp.zeros((BLOCK, BLOCK), jnp.float32)
            for index, value in enumerate(diagonals):
                total = jnp.where(down == index, value, total)
            keep("diagonals", total)
            keep("unused", jnp.zeros((BLOCK, BLOCK), jnp.float32))


def gram_blocks(slab):
    shape = jax.ShapeDtypeStruct((HALF_ROWS, BLOCK), jnp.float32)
    return pl.pallas_call(
        gram_kernel,
        out_shape=(shape, shape),
        in_specs=[pl.BlockSpec(memory_space=pltpu.VMEM)],
        out_specs=(pl.BlockSpec(memory_space=pltpu.VMEM),) * 2,
        compiler_params=pltpu.CompilerParams(vmem_limit_bytes=32 * 2**20),
    )(slab)


def spread(value, sublane):
    return jnp.broadcast_to(value[sublane : sublane + 1], (8, BLOCK))


def eliminate(row, offset, out, beside=None):
    groups = BASE // 8
    lane = iota((8, BLOCK), 1)
    sub = iota((8, BLOCK), 0)
    result = [row[8 * group : 8 * group + 8] for group in range(groups)]

    def copied(start):
        return {
            column: [
                None
                if group < column // 8
                else jnp.broadcast_to(
                    result[group][:, offset + column : offset + column + 1], (8, BLOCK)
                )
                for group in range(groups)
            ]
            for column in range(start, start + GROUP)
        }

    pivots = [jnp.ones((8, BLOCK), jnp.float32) for _ in range(groups)]
    columns = copied(0)
    waiting = []
    if beside is not None:
        beside = [beside[8 * group : 8 * group + 8] for group in range(groups)]

    def follow():
        home, sublane, factors = waiting.pop(0)
        source = spread(beside[home], sublane)
        for group, factor in factors.items():
            beside[group] = beside[group] - factor * source

    for column in range(BASE):
        home, sublane = divmod(column, 8)
        current = columns.pop(column)
        pivot = spread(current[home], sublane)
        inverse_pivot = 1.0 / pivot
        pivots[home] = jnp.where(sub == sublane, pivot, pivots[home])
        scaled = {group: current[group] * inverse_pivot for group in range(home, groups)}
        for later, values in columns.items():
            factor = spread(current[later // 8], later % 8)
            for group in range(later // 8, groups):
                values[group] = values[group] - scaled[group] * factor
        here = lane == offset + column
        source = jnp.where(here, 1.0, spread(result[home], sublane))
        for group in range(home, groups):
            if group == home:
                kept = jnp.where(here, jnp.where(sub == sublane, 1.0, 0.0), result[group])
                if sublane < 7:
                    scaled[group] = jnp.where(sub > sublane, scaled[group], 0.0)
                    kept = kept - scaled[group] * source
                else:
                    del scaled[group]
                result[group] = kept
            else:
                kept = jnp.where(here, 0.0, result[group])
                result[group] = kept - scaled[group] * source
        if column % GROUP == AHEAD and column - AHEAD + GROUP < BASE:
            columns.update(copied(column - AHEAD + GROUP))
        if beside is not None:
            waiting.append((home, sublane, scaled))
            for _ in range(FOLLOW):
                if column >= LATER and waiting:
                    follow()
        yield
    while waiting:
        follow()
    for group in range(groups):
        upper = (lane > sub + (offset + 8 * group)) & (lane < offset + BASE)
        kept = jnp.where(upper, 0.0, result[group])
        scale = lax.rsqrt(pivots[group])
        out.append(kept * scale)
        if beside is not None:
            beside[group] = beside[group] * scale
    if beside is not None:
        out.append(jnp.concatenate(beside, axis=0))


def factor_block(block, beside, beyond, out):
    count = BLOCK // BASE
    rows = [block[BASE * index : BASE * (index + 1)] for index in range(count)]
    lane = iota((BASE, BLOCK), 1)
    inverse, panel, following, below = [], [], None, None
    for index in range(count):
        done = []
        yield from eliminate(rows[index], BASE * index, done, below)
        piece = done.pop() if below is not None else None
        done = jnp.concatenate(done, axis=0)
        start, stop = BASE * index, BASE * (index + 1)
        inverse.append(jnp.where(lane < stop, done, 0.0))
        if index + 1 < count:
            done_parts = split(done)
            change = dot_tn(left_terms(done_parts, 0), right_terms(done_parts, 0))
            for later in range(index + 1, count):
                kept = jnp.where((lane >= start) & (lane < stop), 0.0, rows[later])
                rows[later] = kept - change[BASE * later : BASE * (later + 1)]
        if beside is not None:
            if index == 0:
                source, following = beside(), beyond()
                piece = dot_nn(
                    left_terms(split(inverse[0][:, :stop]), 1),
                    right_terms(split(source[:stop]), 0),
                )
            parts = split(piece)
            if index == 0:
                change = dot_tn(left_terms(done_parts, 0), right_terms(parts, 0))
                below = source[stop:] - change[stop:]
            following = following - dot_tn(left_terms(parts, 0), right_terms(parts, 0))
            panel.append(piece)
        yield
    out.append(jnp.concatenate(inverse, axis=0))
    out.append(jnp.concatenate(panel, axis=0) if panel else None)
    out.append(following)


def weave(steps, tasks):
    count = (BLOCK // BASE) * (BASE + 1)
    done = 0
    for place, _ in enumerate(steps):
        while done < len(tasks) and done * count < (place + 1) * len(tasks):
            tasks[done]()
            done += 1
    while done < len(tasks):
        tasks[done]()
        done += 1


def block_slice(start, stop=None):
    return slice(BLOCK * start, BLOCK * (start + 1 if stop is None else stop))


def step_kernel(
    weights_ref, mine_ref, other_ref, slab_ref, out_ref, check_ref,
    matrix, panel, panel_parts, left_parts, solved, checksum, checked,
):
    low_core = lax.axis_index("core") == 0
    first, second, scale = weights_ref[0], weights_ref[1], weights_ref[2]
    across, down = iota((BLOCK, BLOCK), 1), iota((BLOCK, BLOCK), 0)
    identity = jnp.where(across == down, 1.0, 0.0)
    places = block_places()
    rows_dev = slab_ref.shape[0]

    def fetch(name, rows=slice(0, BLOCK)):
        half, place = places[name]
        here = slice(place * BLOCK + rows.start, place * BLOCK + rows.stop)
        return jnp.where(low_core == (half == 0), mine_ref[here, :], other_ref[here, :]) * scale

    def load(row, column):
        value = fetch((row, column))
        if row == column:
            turned = value.T
            extra = fetch("diagonals", slice(row // 2, row // 2 + 1))
            odd = jnp.where(across < down, value, jnp.where(across > down, turned, extra))
            value = jnp.where(across >= down, value, turned) + identity
            matrix[block_slice(row + 1), block_slice(row + 1)] = odd + identity
        matrix[block_slice(row), block_slice(column)] = value

    def sum_rows(start, stop):
        here = block_slice(start, stop)
        total = jnp.sum(slab_ref[:, here].astype(jnp.float32), axis=0, keepdims=True)
        checksum[:, here] = total / (rows_dev**0.5)

    def keep_panel(start, value):
        here = slice(BLOCK * start, BLOCK * start + value.shape[1])
        panel[:, here] = value
        for index, part in enumerate(split(value)):
            panel_parts[block_slice(index), here] = part

    def make_panel(index, inverse_parts, start, stop):
        source = right_terms(split(matrix[block_slice(index), block_slice(start, stop)]), 0)
        keep_panel(start, dot_nn(inverse_parts, source))

    def turn_panel(row):
        for index, part in enumerate(split(panel[:, block_slice(row)].T)):
            left_parts[block_slice(row), block_slice(index)] = part

    def product(row, row_stop, start, stop):
        rows, columns = block_slice(row, row_stop), block_slice(start, stop)
        left = left_terms([left_parts[rows, block_slice(index)] for index in range(3)], 1)
        right = right_terms([panel_parts[block_slice(index), columns] for index in range(3)], 0)
        return dot_nn(left, right)

    def update_right(index, start, stop):
        rows, columns = block_slice(index + 1, stop), block_slice(start, stop)
        matrix[rows, columns] = matrix[rows, columns] - product(index + 1, stop, start, stop)

    def update_left(index, start, stop):
        change = product(index + 1, COUNT, start, stop)
        rows = block_slice(index + 1, COUNT)
        known = min(stop, index)
        width = BLOCK * (known - start)
        if known > start:
            columns = block_slice(start, known)
            matrix[rows, columns] = matrix[rows, columns] - change[:, :width]
        if stop > index:
            matrix[rows, block_slice(index)] = -change[:, width:]

    def project(index, held):
        columns = block_slice(0, index + 1)
        held.append(
            dot_nt(slab_ref[:, columns], panel_parts[:BLOCK, columns]).astype(jnp.bfloat16)
        )

    def solve(index, held, start, stop):
        columns = block_slice(start, stop)
        value = dot_nn(held[0], panel_parts[:BLOCK, columns])
        width = BLOCK * (min(stop, index) - start)
        if width > 0:
            known = solved[:, BLOCK * start : BLOCK * start + width] + value[:, :width]
            value = jnp.concatenate([known, value[:, width:]], axis=1) if stop > index else known
        if index + 1 == COUNT:
            out_ref[:, columns] = first * slab_ref[:, columns].astype(jnp.float32) + second * value
        else:
            solved[:, columns] = value

    def check(index):
        columns = block_slice(0, index + 1)
        inverse = panel[:, columns]
        weight = jnp.sum(inverse * checksum[:, columns], axis=1, keepdims=True)
        change = (inverse * weight).reshape(BLOCK // 8, 8, inverse.shape[1]).sum(axis=0)
        if index:
            known = block_slice(0, index)
            checked[:, known] = checked[:, known] + change[:, : BLOCK * index]
        checked[:, block_slice(index)] = change[:, BLOCK * index :]

    tasks = []

    def later(function, *arguments):
        tasks.append(lambda: function(*arguments))

    load(0, 0)
    pairs = [name for name in places if isinstance(name, tuple) and name != (0, 0)]
    for pair in sorted(pairs):
        later(load, *pair)
    for start in range(0, COUNT, 2):
        later(sum_rows, start, start + 2)
    diagonal = matrix[block_slice(0), block_slice(0)]
    for index in range(COUNT):
        beside = beyond = None
        if index + 1 < COUNT:
            beside = lambda at=index: matrix[block_slice(at), block_slice(at + 1)]
            beyond = lambda at=index: matrix[block_slice(at + 1), block_slice(at + 1)]
        found = []
        weave(factor_block(diagonal, beside, beyond, found), tasks)
        inverse, neighbour, diagonal = found
        inverse_parts = left_terms(split(inverse), 1)
        tasks = []
        keep_panel(index, inverse)
        if neighbour is not None:
            keep_panel(index + 1, neighbour)
            later(turn_panel, index + 1)
            start = index + 2
            while start < COUNT:
                stop = start + 2 - start % 2
                later(make_panel, index, inverse_parts, start, stop)
                for row in range(start, stop):
                    later(turn_panel, row)
                later(update_right, index, start, stop)
                start = stop
        for start in range(0, index, 2):
            later(make_panel, index, inverse_parts, start, min(start + 2, index))
        if index + 1 < COUNT:
            for start in range(0, index + 1, 2):
                later(update_left, index, start, min(start + 2, index + 1))
        held = []
        later(project, index, held)
        for start in range(0, index + 1, 2):
            later(solve, index, held, start, min(start + 2, index + 1))
        later(check, index)
    for task in tasks:
        task()
    check_ref[...] = first * checksum[...] + second * jnp.sum(checked[...], axis=0, keepdims=True)


def polar_step(weights, mine, other, slab):
    rows_dev = slab.shape[0]
    vmem = pl.BlockSpec(memory_space=pltpu.VMEM)
    return pl.pallas_call(
        step_kernel,
        out_shape=(
            jax.ShapeDtypeStruct((rows_dev, WIDTH), jnp.float32),
            jax.ShapeDtypeStruct((1, WIDTH), jnp.float32),
        ),
        in_specs=[pl.BlockSpec(memory_space=pltpu.SMEM), vmem, vmem, vmem],
        out_specs=(vmem, vmem),
        scratch_shapes=[
            pltpu.VMEM((WIDTH, WIDTH), jnp.float32),
            pltpu.VMEM((BLOCK, WIDTH), jnp.float32),
            pltpu.VMEM((3 * BLOCK, WIDTH), jnp.bfloat16),
            pltpu.VMEM((WIDTH, 3 * BLOCK), jnp.bfloat16),
            pltpu.VMEM((rows_dev, WIDTH), jnp.float32),
            pltpu.VMEM((1, WIDTH), jnp.float32),
            pltpu.VMEM((8, WIDTH), jnp.float32),
        ],
        compiler_params=pltpu.CompilerParams(vmem_limit_bytes=48 * 2**20),
    )(weights, mine, other, slab)


def exchange(parts, axis):
    return lax.all_to_all(parts, axis, 0, 0, tiled=True)


def shared(part, count):
    return jnp.broadcast_to(part[None], (count,) + part.shape)


def swap(value):
    return lax.ppermute(value, "core", [(0, 1), (1, 0)])


def sum_over_devices(mine, other):
    near = ("x", "y_low", "z_low")
    count = 1
    for name in near:
        count *= lax.axis_size(name)
    own = mine + swap(other)
    own = exchange(own.reshape(count, -1, BLOCK), near).sum(axis=0)
    for name in ("y_high", "z_high"):
        own = exchange(shared(own, lax.axis_size(name)), name).sum(axis=0)
    own = exchange(shared(own, count), near).reshape(-1, BLOCK)
    return own, swap(own)


def per_device(slab, lower_bound):
    devices_all = 1
    for name in AXES:
        devices_all *= lax.axis_size(name)
    first, second, shift = qdwh_weights(lower_bound)
    weights = jnp.stack([first, second, shift / (slab.shape[0] * devices_all)])
    mine, other = sum_over_devices(*gram_blocks(slab))
    return polar_step(weights, mine, other, slab)


def solution(mesh):
    wide = Mesh(mesh.devices.reshape(4, 2, 4, 4, 2, 2), AXES)
    return jax.shard_map(
        per_device,
        mesh=wide,
        in_specs=(P(AXES, None), P()),
        out_specs=(P(AXES, None), P(AXES, None)),
        check_vma=False,
    )
```
